256 devices in a mesh: gx: 8 (over x, core), gy: 32 (over y, z).
Axes of the slice: x: 4, y: 4, z: 8, core: 2. Of those that a mesh axis runs over, the one named last changes fastest.
Arguments:
- leaf_multipoles: bfloat16 [32, 128, 16, 128], P('gx', 'gy'), may hold values from -6 to 6
- top_local: float32 [2, 8, 1, 128], replicated, may hold values from -6 to 6
- upward_ops: bfloat16 [1024, 128], replicated, may hold values from -0.1875 to 0.1875
- downward_ops: bfloat16 [128, 1024], replicated, may hold values from -0.5 to 0.5
- translate_ops: bfloat16 [316, 128, 128], replicated, may hold values from -0.0390625 to 0.0390625
- interaction_leaf: int32 [316, 32, 128, 16], P(None, 'gx', 'gy'), may hold values from 0 to 1, as said below
- interaction_one: int32 [316, 16, 64, 8], P(None, 'gx', 'gy'), may hold values from 0 to 1, as said below
- interaction_two: int32 [316, 8, 32, 4], P(None, 'gx', 'gy'), may hold values from 0 to 1, as said below
- interaction_three: int32 [316, 4, 16, 2], replicated, may hold values from 0 to 1, as said below
Outputs:
- leaf_local: float32 [32, 128, 16, 128], P('gx', 'gy')
- top_multipoles: bfloat16 [2, 8, 1, 128], replicated
The draws below stay inside these ranges and needn't reach their ends.
Inputs may be any that keep to these rules, and one draw needn't show every extreme that they name: interaction_leaf[k, b] is 1 exactly when box b and the box at b + offset k are both occupied, lie in the grid, and the latter is a child of a neighbour of b's parent (or of that parent) without touching b; occupied boxes are drawn afresh. `interaction_one`: the same rule at level one, a box being occupied when one of its children is. `interaction_two`: the same rule at level two. `interaction_three`: the same rule at level three.
All inputs are finite; a program needn't handle non-finite values.
Results may differ from the reference program's by a relative error of at most 0.0075.
Values may be sent and summed in bfloat16 or wider, within the bound.
No kernel may reach another device: no remote copies, remote signals or barrier semaphores. Data moves between devices by JAX's collectives and lax.ppermute only.
A program may use at most 256 MiB of HBM per device.

```python
import jax
import jax.numpy as jnp
import numpy as np

COEF = 128
NOFF = 316
NX = 32
NY = 128
NZ = 16


def refine(coarse):
    return jnp.repeat(jnp.repeat(jnp.repeat(coarse, 2, axis=0), 2, axis=1), 2, axis=2)


def occupied_levels(key):
    key_three, key_two, key_one, key_leaf = jax.random.split(key, 4)
    mask_three = (jax.random.randint(key_three, (NX // 8, NY // 8, NZ // 8), 0, 5) < 4).astype(jnp.int32)
    mask_two = (jax.random.randint(key_two, (NX // 4, NY // 4, NZ // 4), 0, 16) < 15).astype(jnp.int32) * refine(mask_three)
    mask_one = (jax.random.randint(key_one, (NX // 2, NY // 2, NZ // 2), 0, 16) < 15).astype(jnp.int32) * refine(mask_two)
    leaf_occupied = (jax.random.randint(key_leaf, (NX, NY, NZ), 0, 8) < 7).astype(jnp.int32) * refine(mask_one)
    levels_all = [leaf_occupied]
    for level_step in range(3):
        finer = levels_all[-1]
        extent_x, extent_y, extent_z = finer.shape
        coarser = finer.reshape(extent_x // 2, 2, extent_y // 2, 2, extent_z // 2, 2).max(axis=(1, 3, 5))
        levels_all.append(coarser)
    return levels_all


def within_reach(shift, parity):
    return ((shift >= -2 - parity) & (shift <= 3 - parity)).astype(jnp.int32)


def interaction_grid(occupied):
    extent_x, extent_y, extent_z = occupied.shape
    padded = jnp.pad(occupied, 3)
    parity_x = (jnp.arange(extent_x, dtype=jnp.int32) % 2)[:, None, None]
    parity_y = (jnp.arange(extent_y, dtype=jnp.int32) % 2)[None, :, None]
    parity_z = (jnp.arange(extent_z, dtype=jnp.int32) % 2)[None, None, :]
    rows_all = []
    for shift_x in range(-3, 4):
        for shift_y in range(-3, 4):
            for shift_z in range(-3, 4):
                if max(abs(shift_x), abs(shift_y), abs(shift_z)) < 2:
                    continue
                allowed = within_reach(shift_x, parity_x) * within_reach(shift_y, parity_y) * within_reach(shift_z, parity_z)
                source = padded[3 + shift_x:3 + shift_x + extent_x, 3 + shift_y:3 + shift_y + extent_y, 3 + shift_z:3 + shift_z + extent_z]
                rows_all.append((allowed * occupied * source).astype(jnp.int32))
    return jnp.stack(rows_all)


def draw_interaction_leaf(key, part):
    return interaction_grid(occupied_levels(key)[0])


def draw_interaction_one(key, part):
    return interaction_grid(occupied_levels(key)[1])


def draw_interaction_two(key, part):
    return interaction_grid(occupied_levels(key)[2])


def draw_interaction_three(key, part):
    return interaction_grid(occupied_levels(key)[3])


def levels(own_key, extent, cuts, low, high):
    loudness = 1.0
    for position, shards_of in cuts:
        draws = jax.random.uniform(jax.random.fold_in(jax.random.fold_in(own_key, 6), position), (shards_of,), jnp.float32, low / len(cuts), high / len(cuts))
        loudness = loudness * jnp.repeat(jnp.exp(draws), extent[position] // shards_of).reshape((-1,) + (1,) * (len(extent) - 1 - position))
    return loudness


def gaussian(stream_key, dims, scale, bound, cuts=(), kind=jnp.bfloat16):
    factor_of = levels(stream_key, dims, cuts, -0.22, 0.18) if cuts else 1.0
    entries = jax.random.normal(stream_key, dims, jnp.float32) * scale * factor_of
    return jnp.minimum(jnp.maximum(entries, -bound), bound).astype(kind)


def setup_inputs(seed: int = 0) -> dict:
    arg_keys = jax.random.split(jax.random.key(seed), 10)
    return {
        "leaf_multipoles": gaussian(arg_keys[0], (NX, NY, NZ, COEF), 1.0, 6.0, ((0, 8), (1, 32))),
        "top_local": gaussian(arg_keys[1], (NX // 16, NY // 16, NZ // 16, COEF), 1.0, 6.0, (), jnp.float32),
        "upward_ops": gaussian(arg_keys[2], (8 * COEF, COEF), (8 * COEF) ** -0.5, 0.1875),
        "downward_ops": gaussian(arg_keys[3], (COEF, 8 * COEF), COEF ** -0.5, 0.5),
        "translate_ops": gaussian(arg_keys[4], (NOFF, COEF, COEF), (189 * COEF) ** -0.5, 0.0390625),
        "interaction_leaf": draw_interaction_leaf(jax.random.fold_in(arg_keys[9], 71), 0),
        "interaction_one": draw_interaction_one(jax.random.fold_in(arg_keys[9], 71), 0),
        "interaction_two": draw_interaction_two(jax.random.fold_in(arg_keys[9], 71), 0),
        "interaction_three": draw_interaction_three(jax.random.fold_in(arg_keys[9], 71), 0),
    }


def offset_table():
    rows_all = []
    for shift_x in range(-3, 4):
        for shift_y in range(-3, 4):
            for shift_z in range(-3, 4):
                if max(abs(shift_x), abs(shift_y), abs(shift_z)) >= 2:
                    rows_all.append((shift_x, shift_y, shift_z))
    return np.array(rows_all, np.int32)


def pad_rim(field):
    return jnp.pad(field, ((3, 3), (3, 3), (3, 3), (0, 0)))


def upward(child, upward_ops):
    extent_x, extent_y, extent_z, coef_width = child.shape
    grouped = child.reshape(extent_x // 2, 2, extent_y // 2, 2, extent_z // 2, 2, coef_width)
    grouped = grouped.transpose(0, 2, 4, 1, 3, 5, 6).reshape(-1, 8 * coef_width)
    parent = jnp.dot(grouped, upward_ops, preferred_element_type=jnp.float32)
    return parent.reshape(extent_x // 2, extent_y // 2, extent_z // 2, coef_width).astype(jnp.bfloat16)


def downward(local_field, downward_ops):
    extent_x, extent_y, extent_z, coef_width = local_field.shape
    rounded = local_field.astype(jnp.bfloat16)
    spread = jnp.dot(rounded.reshape(-1, coef_width), downward_ops, preferred_element_type=jnp.float32)
    spread = spread.reshape(extent_x, extent_y, extent_z, 2, 2, 2, coef_width)
    return spread.transpose(0, 3, 1, 4, 2, 5, 6).reshape(2 * extent_x, 2 * extent_y, 2 * extent_z, coef_width)


def m2l_sum(padded, lists, translate_ops, level_scale, group_size):
    extent_x = padded.shape[0] - 6
    extent_y = padded.shape[1] - 6
    extent_z = padded.shape[2] - 6
    coef_width = padded.shape[3]
    offsets_all = offset_table()
    offset_count = offsets_all.shape[0]
    summed = jnp.zeros((extent_x * extent_y * extent_z, coef_width), jnp.float32)
    for first_id in range(0, offset_count, group_size):
        last_id = min(first_id + group_size, offset_count)
        pieces = []
        for offset in range(first_id, last_id):
            shift_x, shift_y, shift_z = (int(value) for value in offsets_all[offset])
            source = padded[3 + shift_x:3 + shift_x + extent_x, 3 + shift_y:3 + shift_y + extent_y, 3 + shift_z:3 + shift_z + extent_z, :]
            mark_cols = lists[offset].astype(jnp.bfloat16)[..., None]
            pieces.append(source * mark_cols)
        stacked = jnp.concatenate(pieces, axis=-1).reshape(-1, (last_id - first_id) * coef_width)
        op_block = translate_ops[first_id:last_id].reshape((last_id - first_id) * coef_width, coef_width)
        summed = summed + jnp.dot(stacked, op_block, preferred_element_type=jnp.float32)
    return (summed * level_scale).reshape(extent_x, extent_y, extent_z, coef_width)


def reference(leaf_multipoles, top_local, upward_ops, downward_ops, translate_ops, interaction_leaf, interaction_one, interaction_two, interaction_three):
    level_one = upward(leaf_multipoles, upward_ops)
    level_two = upward(level_one, upward_ops)
    level_three = upward(level_two, upward_ops)
    top_multipoles = upward(level_three, upward_ops)
    local_three = downward(top_local, downward_ops) + m2l_sum(pad_rim(level_three), interaction_three, translate_ops, 0.125, 4)
    local_two = downward(local_three, downward_ops) + m2l_sum(pad_rim(level_two), interaction_two, translate_ops, 0.25, 4)
    local_one = downward(local_two, downward_ops) + m2l_sum(pad_rim(level_one), interaction_one, translate_ops, 0.5, 4)
    leaf_local = downward(local_one, downward_ops) + m2l_sum(pad_rim(leaf_multipoles), interaction_leaf, translate_ops, 1.0, 4)
    return leaf_local, top_multipoles
```

```python
import functools

import jax
import jax.numpy as jnp
from jax import lax
from jax.experimental import pallas as pl
from jax.experimental.pallas import tpu as pltpu
from jax.sharding import PartitionSpec as P

F32 = jnp.float32
BF16 = jnp.bfloat16
COEF = 128
PAIR = 256
NOFF = 316
VM = pltpu.VMEM
ANY_SPEC = pl.BlockSpec(memory_space=pl.ANY)
VMEM_SPEC = pl.BlockSpec(memory_space=pltpu.VMEM)

PLANE_FIRST = (0, 49, 98, 138, 178, 218, 267)
PLANE_COUNT = (49, 49, 40, 40, 40, 49, 49)
THIN_FIRST = (0, 7, 14, 18, 22, 26, 33)


def dot(lhs, rhs):
    return jnp.dot(lhs, rhs, preferred_element_type=F32)


def prepare_kernel(
    leaf_ref, up_ref, list_leaf_ref, list_one_ref,
    leaf_out, leaf_mask_out, one_out, one_mask_out, even_out, odd_out, two_out,
    raw, masked, marks, one_raw, one_masked, one_marks, pairs, two_in,
):
    parity = lax.axis_index("gx") % 2
    for x in range(4):
        for y in range(4):
            rows = pl.ds((x * 4 + y) * 16, 16)
            flags = list_leaf_ref[x, y].astype(F32)
            mark = jnp.broadcast_to(jnp.max(flags, axis=1, keepdims=True), (16, COEF))
            value = leaf_ref[x, y].astype(F32)
            raw[rows, :] = value
            masked[rows, :] = value * mark
            marks[rows, :] = mark
    cols = []
    for p in range(2):
        for q in range(2):
            for r in range(2):
                parts = []
                for x in range(2):
                    for y in range(2):
                        first = ((2 * x + p) * 4 + 2 * y + q) * 16 + r
                        parts.append(raw[pl.ds(first, 8, stride=2), :])
                cols.append(jnp.concatenate(parts, axis=0).astype(BF16))
    level_one = dot(jnp.concatenate(cols, axis=1), up_ref[...]).astype(BF16).astype(F32)
    one_raw[...] = level_one
    for x in range(2):
        for y in range(2):
            rows = pl.ds((x * 2 + y) * 8, 8)
            flags = list_one_ref[x, y].astype(F32)
            mark = jnp.broadcast_to(jnp.max(flags, axis=1, keepdims=True), (8, COEF))
            one_masked[rows, :] = one_raw[rows, :] * mark
            one_marks[rows, :] = mark
    two_in[...] = jnp.zeros_like(two_in)
    for p in range(2):
        for q in range(2):
            for r in range(2):
                first = (p * 2 + q) * 8 + r
                lane = (4 * p + 2 * q + r) * COEF
                two_in[0:4, lane:lane + COEF] = one_raw[pl.ds(first, 4, stride=2), :]
    level_two = dot(two_in[...].astype(BF16), up_ref[...])
    two_out[...] = level_two[0:4, :].astype(BF16)
    for x in range(4):
        for half in range(2):
            for r in range(2):
                lane = r * COEF
                parts = []
                part_marks = []
                for y in (2 * half, 2 * half + 1):
                    first = (x * 4 + y) * 16 + r
                    parts.append(masked[pl.ds(first, 8, stride=2), :])
                    part_marks.append(marks[pl.ds(first, 8, stride=2), :])
                rows = slice(half * 16, half * 16 + 16)
                leaf_out[x, rows, lane:lane + COEF] = jnp.concatenate(parts, axis=0).astype(BF16)
                leaf_mask_out[x, rows, lane:lane + COEF] = jnp.concatenate(part_marks, axis=0)
    for column in range(4):
        for r in range(2):
            lane = r * COEF
            rows = slice(column * 4, column * 4 + 4)
            pairs[rows, lane:lane + COEF] = one_masked[pl.ds(column * 8 + r, 4, stride=2), :]
            one_mask_out[rows, lane:lane + COEF] = one_marks[pl.ds(column * 8 + r, 4, stride=2), :]
    one_pairs = pairs[...].astype(BF16)
    one_out[...] = one_pairs
    for x in range(2):
        even_out[x * 32:x * 32 + 32, :] = leaf_out[2 * (1 - parity) + x]
        odd_out[x * 32:x * 32 + 32, :] = leaf_out[2 * parity + x]
    even_out[64:80, :] = one_pairs
    odd_out[64:80, :] = one_pairs


def prepare(leaf, upward_ops, list_leaf, list_one):
    return pl.pallas_call(
        prepare_kernel,
        out_shape=(
            jax.ShapeDtypeStruct((4, 32, PAIR), BF16),
            jax.ShapeDtypeStruct((4, 32, PAIR), F32),
            jax.ShapeDtypeStruct((16, PAIR), BF16),
            jax.ShapeDtypeStruct((16, PAIR), F32),
            jax.ShapeDtypeStruct((80, PAIR), BF16),
            jax.ShapeDtypeStruct((80, PAIR), BF16),
            jax.ShapeDtypeStruct((4, COEF), BF16),
        ),
        in_specs=[VMEM_SPEC] * 4,
        out_specs=[VMEM_SPEC] * 7,
        scratch_shapes=[
            VM((256, COEF), F32),
            VM((256, COEF), F32),
            VM((256, COEF), F32),
            VM((32, COEF), F32),
            VM((32, COEF), F32),
            VM((32, COEF), F32),
            VM((16, PAIR), F32),
            VM((8, 1024), F32),
        ],
        compiler_params=pltpu.CompilerParams(vmem_limit_bytes=16 * 2**20),
        name="prepare",
    )(leaf, upward_ops, list_leaf, list_one)


def forward_kernel(leaf_ref, one_ref, even_ref, odd_ref, even_out, odd_out):
    parity = lax.axis_index("gy") % 2
    for out, side in ((even_out, 1 - parity), (odd_out, parity)):
        rows = pl.ds(pl.multiple_of(side * 16, 16), 16)
        for x in range(4):
            out[x * 16:x * 16 + 16, :] = leaf_ref[x, rows, :]
        out[64:80, :] = one_ref[...]
        for place, got in enumerate((even_ref, odd_ref)):
            first = 80 + 48 * place
            for x in range(2):
                face = pl.ds(pl.multiple_of(x * 32 + side * 16, 16), 16)
                out[first + x * 16:first + x * 16 + 16, :] = got[face, :]
            out[first + 32:first + 48, :] = got[64:80, :]


def forward(leaf, one, even, odd):
    return pl.pallas_call(
        forward_kernel,
        out_shape=(jax.ShapeDtypeStruct((176, PAIR), BF16),) * 2,
        in_specs=[VMEM_SPEC] * 4,
        out_specs=[VMEM_SPEC] * 2,
        compiler_params=pltpu.CompilerParams(vmem_limit_bytes=4 * 2**20),
        name="forward",
    )(leaf, one, even, odd)


def lane_of(plane, b, c):
    if plane in (2, 3, 4) and -1 <= b <= 1:
        return PLANE_FIRST[plane] + THIN_FIRST[b + 3] + {-3: 0, -2: 1, -1: 2, 2: 2, 3: 3}[c]
    first = THIN_FIRST[b + 3] if plane in (2, 3, 4) else 7 * (b + 3)
    return PLANE_FIRST[plane] + first + c + 3


def window_of(window, one_window, leaf_ref, one_ref, evenx_ref, oddx_ref, eveny_ref, oddy_ref):
    parity_x = lax.axis_index("gx") % 2
    parity_y = lax.axis_index("gy") % 2
    even_x, odd_x = 6 * (1 - parity_x), 6 * parity_x
    even_y, odd_y = 6 * (1 - parity_y), 6 * parity_y
    one_even_x, one_odd_x = 1 + 4 * (1 - parity_x), 1 + 4 * parity_x
    one_even_y, one_odd_y = 1 + 4 * (1 - parity_y), 1 + 4 * parity_y

    def put(x, y, block):
        block = block.astype(F32)
        window[x, y, 8:16, :] = block[0:8]
        window[x, y + 1, 8:16, :] = block[8:16]

    def put_one(x, y, block):
        block = block.astype(F32)
        for i in range(2):
            for j in range(2):
                first = (2 * i + j) * 4
                one_window[x + i, y + j, 8:12, :] = block[first:first + 4]

    for x in range(4):
        put(2 + x, 2, leaf_ref[x, 0:16, :])
        put(2 + x, 4, leaf_ref[x, 16:32, :])
    put_one(3, 3, one_ref[...])
    for got, place, one_place in ((evenx_ref, even_x, one_even_x), (oddx_ref, odd_x, one_odd_x)):
        for x in range(2):
            put(place + x, 2, got[x * 32:x * 32 + 16, :])
            put(place + x, 4, got[x * 32 + 16:x * 32 + 32, :])
        put_one(one_place, 3, got[64:80, :])
    for got, y, one_y in ((eveny_ref, even_y, one_even_y), (oddy_ref, odd_y, one_odd_y)):
        for x in range(4):
            put(2 + x, y, got[x * 16:x * 16 + 16, :])
        put_one(3, one_y, got[64:80, :])
        for first, place, one_place in ((80, even_x, one_even_x), (128, odd_x, one_odd_x)):
            for x in range(2):
                put(place + x, y, got[first + x * 16:first + x * 16 + 16, :])
            put_one(one_place, one_y, got[first + 32:first + 48, :])


def translate_kernel(
    leaf_ref, leaf_mask_ref, one_ref, one_mask_ref, evenx_ref, oddx_ref, eveny_ref, oddy_ref,
    two_ref, up_ref, down_ref, top_ref, list_two_ref, list_three_ref, ops_hbm,
    out_ref, top_out,
    ops, window, one_window, chunks, one_chunks, high_chunks, two_rows, three_rows, acc,
    flags, one_local, sems,
):
    gx = lax.axis_index("gx")
    gy = lax.axis_index("gy")
    copies = []
    for plane in range(7):
        span = pl.ds(PLANE_FIRST[plane], PLANE_COUNT[plane])
        copies.append(pltpu.make_async_copy(ops_hbm.at[span], ops.at[span], sems.at[plane]))
        copies[-1].start()

    window[:, :, 0:8, :] = jnp.zeros((8, 8, 8, PAIR), F32)
    window[:, :, 16:24, :] = jnp.zeros((8, 8, 8, PAIR), F32)
    one_window[...] = jnp.zeros_like(one_window)
    window_of(window, one_window, leaf_ref, one_ref, evenx_ref, oddx_ref, eveny_ref, oddy_ref)
    chunks[...] = jnp.zeros_like(chunks)

    def fill(x, carry):
        for q in range(2):
            for d in range(3):
                for shift in range(3):
                    rows = pl.ds(7 + shift, 8)
                    both = [window[x, 2 * (y + d) + q, rows, :] for y in range(2)]
                    chunks[x, 3 * q + d, shift] = jnp.concatenate(both, axis=0).astype(BF16)
        return carry

    lax.fori_loop(0, 8, fill, 0)

    two_rows[...] = two_ref[...].astype(F32)
    cols = []
    for p in range(2):
        for q in range(2):
            for r in range(2):
                parts = []
                for x in range(4):
                    for z in range(2):
                        first = (2 * x + p) * 128 + q * 4 + 2 * z + r
                        parts.append(two_rows[pl.ds(first, 16, stride=8), :])
                cols.append(jnp.concatenate(parts, axis=0).astype(BF16))
    level_three = dot(jnp.concatenate(cols, axis=1), up_ref[...])
    three_rows[...] = level_three.astype(BF16).astype(F32)
    cols = []
    for p in range(2):
        for q in range(2):
            for r in range(2):
                parts = []
                for x in range(2):
                    first = ((2 * x + p) * 2 + r) * 16 + q
                    parts.append(three_rows[pl.ds(first, 8, stride=2), :])
                cols.append(jnp.concatenate(parts, axis=0).astype(BF16))
    top_out[...] = dot(jnp.concatenate(cols, axis=1), up_ref[...]).astype(BF16)

    three_x, three_y = gx // 2, gy // 2
    flags[...] = jnp.zeros_like(flags)
    flags[0:4, :] = list_two_ref[...].astype(F32)
    flags[4:6, :] = list_three_ref[three_x, three_y].astype(F32)
    row = lax.broadcasted_iota(jnp.int32, (8, NOFF), 0)
    held = flags[...]
    moved = jnp.concatenate([jnp.zeros((8, 1), F32), held[:, :NOFF - 1]], axis=1)
    marked = jnp.where(row % 2 == 0, held, moved)
    row = lax.broadcasted_iota(jnp.int32, (8, COEF), 0)
    for plane in range(7):
        two_x = jnp.clip(gx + plane - 3, 0, 7)
        far_x = jnp.clip(three_x + plane - 3, 0, 3)
        for b in range(-3, 4):
            two_first = (two_x * 32 + jnp.clip(gy + b, 0, 31)) * 4
            far_first = far_x * 32 + jnp.clip(three_y + b, 0, 15)
            thin = plane in (2, 3, 4) and -1 <= b <= 1
            for r in range(2):
                low = two_rows[pl.ds(two_first + r, 1), :]
                high = two_rows[pl.ds(two_first + 2 + r, 1), :]
                far = three_rows[pl.ds(far_first + 16 * r, 1), :]
                low, high, far = (jnp.broadcast_to(v, (8, COEF)) for v in (low, high, far))
                near = jnp.where(row < 2, low, jnp.where(row < 4, high, far))
                for shift in range(3):
                    if thin and shift == 1:
                        continue
                    lane = lane_of(plane, b, 2 * (shift - 1) + r)
                    mark = jnp.broadcast_to(marked[:, lane:lane + 1], (8, COEF))
                    if shift == 0:
                        value = low
                    elif shift == 2:
                        value = high
                    else:
                        value = near
                    value = jnp.concatenate([value * mark, jnp.zeros((8, COEF), F32)], axis=0)
                    high_chunks[plane * 7 + b + 3, shift, :, r * COEF:r * COEF + COEF] = (
                        value.astype(BF16)
                    )

    acc[...] = jnp.zeros_like(acc)
    zero = jnp.zeros((COEF, COEF), BF16)

    def plane_step(plane, first, thin_plane):
        a = plane - 3
        places = []
        for px in range(2):
            good = (a >= -2) if px == 0 else (a <= 2)
            for x in range(2):
                places.append(jnp.where(good, 2 * x + px + a + 2, 8))
        for b in range(-3, 4):
            for shift in range(3):
                for px in range(2):
                    for py in range(2):
                        rows = slice((2 * px + py) * 4, (2 * px + py) * 4 + 4)
                        one_chunks[b + 3, shift, rows, :] = one_window[
                            px + a + 3, py + b + 3, 7 + shift:11 + shift, :
                        ]
        total = None
        for b in range(-3, 4):
            thin = thin_plane and -1 <= b <= 1
            start = first + (THIN_FIRST[b + 3] if thin_plane else 7 * (b + 3))
            shifts = (0, 2) if thin else (0, 1, 2)
            left = []
            right = []
            for shift in shifts:
                blocks = []
                for px in range(2):
                    for py in range(2):
                        y = py + b
                        good = (b >= -2) if py == 0 else (b <= 2)
                        q, d = y % 2, y // 2 + 1
                        for x in range(2):
                            if good:
                                blocks.append(chunks[places[2 * px + x], 3 * q + d, shift])
                            else:
                                blocks.append(jnp.zeros((16, PAIR), BF16))
                blocks.append(one_chunks[b + 3, shift].astype(BF16))
                blocks.append(high_chunks[plane * 7 + b + 3, shift])
                left.append(jnp.concatenate(blocks, axis=0))
                if thin:
                    if shift == 0:
                        same, prev, after = ops[start + 1], ops[start], zero
                    else:
                        same, prev, after = ops[start + 2], zero, ops[start + 3]
                else:
                    c = 2 * (shift - 1) + 3
                    same, prev, after = ops[start + c], ops[start + c - 1], ops[start + c + 1]
                right.append(jnp.concatenate([same, prev], axis=1))
                right.append(jnp.concatenate([after, same], axis=1))
            product = dot(jnp.concatenate(left, axis=1), jnp.concatenate(right, axis=0))
            total = product if total is None else total + product
        acc[...] = acc[...] + total

    def wide_step(i, carry):
        plane = jnp.where(i < 2, i, i + 3)
        first = jnp.where(i < 2, 49 * i, 49 * i + 120)
        span = pl.ds(first, 49)
        pltpu.make_async_copy(ops_hbm.at[span], ops.at[span], sems.at[plane]).wait()
        plane_step(plane, first, False)
        return carry

    def thin_step(i, carry):
        first = 98 + 40 * i
        span = pl.ds(first, 40)
        pltpu.make_async_copy(ops_hbm.at[span], ops.at[span], sems.at[i + 2]).wait()
        plane_step(i + 2, first, True)
        return carry

    lax.fori_loop(0, 3, thin_step, 0)
    lax.fori_loop(0, 4, wide_step, 0)

    high = acc[144:152, :]
    top_x, top_y = three_x // 2, three_y // 2
    column = pl.multiple_of((three_x % 2 * 4 + three_y % 2 * 2) * COEF, PAIR)
    top_row = jnp.broadcast_to(top_ref[top_x, top_y], (8, COEF)).astype(BF16)
    three = dot(top_row, down_ref[:, pl.ds(column, PAIR)])
    row = lax.broadcasted_iota(jnp.int32, (8, COEF), 0)
    three_low = three[0:1, 0:COEF] + high[4:5, 0:COEF] * 0.125
    three_high = three[0:1, COEF:PAIR] + high[5:6, COEF:PAIR] * 0.125
    local_three = jnp.where(
        row == 0, jnp.broadcast_to(three_low, (8, COEF)), jnp.broadcast_to(three_high, (8, COEF))
    )
    column = pl.multiple_of((gx % 2 * 4 + gy % 2 * 2) * COEF, PAIR)
    two = dot(local_three.astype(BF16), down_ref[:, pl.ds(column, PAIR)])
    local_two = None
    for z in range(4):
        lanes = slice((z % 2) * COEF, (z % 2) * COEF + COEF)
        value = two[z // 2:z // 2 + 1, lanes] + high[z:z + 1, lanes] * 0.25
        value = jnp.broadcast_to(value, (8, COEF))
        local_two = value if local_two is None else jnp.where(row >= z, value, local_two)
    one = dot(local_two.astype(BF16), down_ref[...])
    for column in range(4):
        rows = slice(column * 4, column * 4 + 4)
        for r in range(2):
            lanes = slice(r * COEF, r * COEF + COEF)
            wide = slice((2 * column + r) * COEF, (2 * column + r) * COEF + COEF)
            far = acc[128 + column * 4:132 + column * 4, lanes] * one_mask_ref[rows, lanes]
            one_local[pl.ds(column * 8 + r, 4, stride=2), :] = one[0:4, wide] + far * 0.5
    leaf = dot(one_local[...].astype(BF16), down_ref[...])
    for px in range(2):
        for py in range(2):
            for x in range(2):
                for y in range(2):
                    part = 8 * (2 * x + y)
                    held = ((2 * px + py) * 2 + x) * 16 + 8 * y
                    box_x, box_y = 2 * x + px, 2 * y + py
                    for r in range(2):
                        lanes = slice(r * COEF, r * COEF + COEF)
                        wide = slice((4 * px + 2 * py + r) * COEF, (4 * px + 2 * py + r + 1) * COEF)
                        mark = leaf_mask_ref[box_x, box_y * 8:box_y * 8 + 8, lanes]
                        out_ref[box_x, box_y, pl.ds(r, 8, stride=2), :] = (
                            leaf[part:part + 8, wide] + acc[held:held + 8, lanes] * mark
                        )


def translate(*operands):
    return pl.pallas_call(
        translate_kernel,
        out_shape=(
            jax.ShapeDtypeStruct((4, 4, 16, COEF), F32),
            jax.ShapeDtypeStruct((16, COEF), BF16),
        ),
        in_specs=[VMEM_SPEC] * 14 + [ANY_SPEC],
        out_specs=[VMEM_SPEC] * 2,
        scratch_shapes=[
            VM((NOFF, COEF, COEF), BF16),
            VM((8, 8, 24, PAIR), F32),
            VM((8, 8, 16, PAIR), F32),
            VM((9, 6, 3, 16, PAIR), BF16),
            VM((7, 3, 16, PAIR), F32),
            VM((49, 3, 16, PAIR), BF16),
            VM((1024, COEF), F32),
            VM((128, COEF), F32),
            VM((160, PAIR), F32),
            VM((8, NOFF), F32),
            VM((32, COEF), F32),
            pltpu.SemaphoreType.DMA((7,)),
        ],
        compiler_params=pltpu.CompilerParams(vmem_limit_bytes=40 * 2**20),
        name="translate",
    )(*operands)


def swaps(count):
    even = [(i, i ^ 1) for i in range(count)]
    odd = [(i, ((i + 1) ^ 1) - 1) for i in range(1, count - 1)]
    return even, odd


def local(
    leaf_multipoles, top_local, upward_ops, downward_ops, translate_ops,
    interaction_leaf, interaction_one, interaction_two, interaction_three,
):
    count_x, count_y = lax.axis_size("gx"), lax.axis_size("gy")
    last = (1, 2, 3, 0)
    leaf, leaf_mask, one, one_mask, to_even, to_odd, two = prepare(
        leaf_multipoles, upward_ops, interaction_leaf.transpose(last), interaction_one.transpose(last)
    )
    even, odd = swaps(count_x)
    even_x = lax.ppermute(to_even, "gx", even)
    odd_x = lax.ppermute(to_odd, "gx", odd)
    to_even, to_odd = forward(leaf, one, even_x, odd_x)
    even, odd = swaps(count_y)
    even_y = lax.ppermute(to_even, "gy", even)
    odd_y = lax.ppermute(to_odd, "gy", odd)
    copies = jnp.broadcast_to(two[None], (count_x * count_y, 4, COEF))
    all_two = lax.all_to_all(copies, ("gx", "gy"), 0, 0, tiled=True).reshape(-1, COEF)
    leaf_local, top = translate(
        leaf, leaf_mask, one, one_mask, even_x, odd_x, even_y, odd_y,
        all_two, upward_ops, downward_ops, top_local,
        interaction_two.transpose(last).reshape(4, NOFF), interaction_three.transpose(last),
        translate_ops,
    )
    return leaf_local, top.reshape(2, 8, 1, COEF)


def solution(mesh):
    return jax.shard_map(
        local,
        mesh=mesh,
        in_specs=(
            P("gx", "gy", None, None),
            P(),
            P(),
            P(),
            P(),
            P(None, "gx", "gy", None),
            P(None, "gx", "gy", None),
            P(None, "gx", "gy", None),
            P(),
        ),
        out_specs=(P("gx", "gy", None, None), P()),
        check_vma=False,
    )
```

```python
import functools

import jax
import jax.numpy as jnp
from jax import lax
from jax.experimental import pallas as pl
from jax.experimental.pallas import tpu as pltpu
from jax.sharding import PartitionSpec as P

F32 = jnp.float32
BF16 = jnp.bfloat16
COEF = 128
PAIR = 256
NOFF = 316
VM = pltpu.VMEM
LIM1 = 60
LIM2 = 60
ANY_SPEC = pl.BlockSpec(memory_space=pl.ANY)
VMEM_SPEC = pl.BlockSpec(memory_space=pltpu.VMEM)

PLANE_FIRST = (0, 49, 98, 138, 178, 218, 267)
PLANE_COUNT = (49, 49, 40, 40, 40, 49, 49)
PLANE_ORDER = (2, 3, 4, 1, 5, 0, 6)
THIN_FIRST = (0, 7, 14, 18, 22, 26, 33)


def fetch(sources, targets, sems):
    copies = []
    for place, (source, target) in enumerate(zip(sources, targets)):
        copies.append(pltpu.make_async_copy(source, target, sems.at[place]))
        copies[-1].start()
    return copies


def dot(lhs, rhs):
    return jnp.dot(lhs, rhs, preferred_element_type=F32)


def prepare_kernel(
    leaf_hbm, up_hbm, list_leaf_hbm, list_one_hbm,
    own_out, even_out, odd_out, two_out,
    leaf_ref, up_ref, list_leaf_ref, list_one_ref,
    raw, masked, marks, one_raw, one_masked, one_marks, pairs, pair_marks, two_in, sems,
):
    copies = fetch(
        (leaf_hbm, list_leaf_hbm, up_hbm, list_one_hbm),
        (leaf_ref, list_leaf_ref, up_ref, list_one_ref),
        sems,
    )
    parity = lax.axis_index("gy") % 2
    copies[0].wait()
    copies[1].wait()
    for x in range(4):
        for y in range(4):
            rows = pl.ds((x * 4 + y) * 16, 16)
            flags = list_leaf_ref[x, y].astype(F32)
            mark = jnp.broadcast_to(jnp.max(flags, axis=1, keepdims=True), (16, COEF))
            value = leaf_ref[x, y].astype(F32)
            raw[rows, :] = value
            masked[rows, :] = value * mark
            marks[rows, :] = mark
    copies[2].wait()
    copies[3].wait()
    cols = []
    for p in range(2):
        for q in range(2):
            for r in range(2):
                parts = []
                for x in range(2):
                    for y in range(2):
                        first = ((2 * x + p) * 4 + 2 * y + q) * 16 + r
                        parts.append(raw[pl.ds(first, 8, stride=2), :])
                cols.append(jnp.concatenate(parts, axis=0).astype(BF16))
    level_one = dot(jnp.concatenate(cols, axis=1), up_ref[...]).astype(BF16).astype(F32)
    one_raw[...] = level_one
    for x in range(2):
        for y in range(2):
            rows = pl.ds((x * 2 + y) * 8, 8)
            flags = list_one_ref[x, y].astype(F32)
            mark = jnp.broadcast_to(jnp.max(flags, axis=1, keepdims=True), (8, COEF))
            one_masked[rows, :] = one_raw[rows, :] * mark
            one_marks[rows, :] = mark
    two_in[...] = jnp.zeros_like(two_in)
    for p in range(2):
        for q in range(2):
            for r in range(2):
                first = (p * 2 + q) * 8 + r
                lane = (4 * p + 2 * q + r) * COEF
                two_in[0:4, lane:lane + COEF] = one_raw[pl.ds(first, 4, stride=2), :]
    level_two = dot(two_in[...].astype(BF16), up_ref[...])
    two_out[...] = jnp.broadcast_to(level_two[0:4, :].astype(BF16)[None], two_out.shape)
    for x in range(4):
        for half in range(2):
            for r in range(2):
                lane = r * COEF
                parts = []
                part_marks = []
                for y in (2 * half, 2 * half + 1):
                    first = (x * 4 + y) * 16 + r
                    parts.append(masked[pl.ds(first, 8, stride=2), :])
                    part_marks.append(marks[pl.ds(first, 8, stride=2), :])
                first = x * 32 + half * 16
                rows = slice(first, first + 16)
                own_out[rows, lane:lane + COEF] = jnp.concatenate(parts, axis=0).astype(BF16)
                rows = slice(144 + first, 160 + first)
                own_out[rows, lane:lane + COEF] = jnp.concatenate(part_marks, axis=0).astype(BF16)
    for column in range(4):
        for r in range(2):
            lane = r * COEF
            rows = slice(column * 4, column * 4 + 4)
            pairs[rows, lane:lane + COEF] = one_masked[pl.ds(column * 8 + r, 4, stride=2), :]
            pair_marks[rows, lane:lane + COEF] = one_marks[pl.ds(column * 8 + r, 4, stride=2), :]
    one_pairs = pairs[...].astype(BF16)
    own_out[128:144, :] = one_pairs
    own_out[272:288, :] = pair_marks[...].astype(BF16)
    for out, side in ((even_out, 1 - parity), (odd_out, parity)):
        for x in range(4):
            rows = pl.ds(pl.multiple_of(x * 32 + side * 16, 16), 16)
            out[x * 16:x * 16 + 16, :] = own_out[rows, :]
    even_out[64:80, :] = one_pairs
    odd_out[64:80, :] = one_pairs


def prepare(receivers, leaf, upward_ops, list_leaf, list_one):
    return pl.pallas_call(
        prepare_kernel,
        out_shape=(
            jax.ShapeDtypeStruct((288, PAIR), BF16),
            jax.ShapeDtypeStruct((80, PAIR), BF16),
            jax.ShapeDtypeStruct((80, PAIR), BF16),
            jax.ShapeDtypeStruct((receivers, 4, COEF), BF16),
        ),
        in_specs=[ANY_SPEC] * 4,
        out_specs=[VMEM_SPEC] * 4,
        scratch_shapes=[
            VM((4, 4, 16, COEF), BF16),
            VM((1024, COEF), BF16),
            VM((4, 4, 16, NOFF), jnp.int32),
            VM((2, 2, 8, NOFF), jnp.int32),
            VM((256, COEF), F32),
            VM((256, COEF), F32),
            VM((256, COEF), F32),
            VM((32, COEF), F32),
            VM((32, COEF), F32),
            VM((32, COEF), F32),
            VM((16, PAIR), F32),
            VM((16, PAIR), F32),
            VM((8, 1024), F32),
            pltpu.SemaphoreType.DMA((4,)),
        ],
        compiler_params=pltpu.CompilerParams(vmem_limit_bytes=int(LIM1 * 2**20)),
        name="prepare",
    )(leaf, upward_ops, list_leaf, list_one)


def forward_kernel(own_ref, even_ref, odd_ref, even_out, odd_out):
    parity = lax.axis_index("gx") % 2
    for out, side in ((even_out, 1 - parity), (odd_out, parity)):
        out[0:64, :] = own_ref[pl.ds(pl.multiple_of(side * 64, 64), 64), :]
        out[64:80, :] = own_ref[128:144, :]
        for first, got in ((80, even_ref), (128, odd_ref)):
            out[first:first + 32, :] = got[pl.ds(pl.multiple_of(side * 32, 32), 32), :]
            out[first + 32:first + 48, :] = got[64:80, :]


def forward(own, even, odd):
    return pl.pallas_call(
        forward_kernel,
        out_shape=(jax.ShapeDtypeStruct((176, PAIR), BF16),) * 2,
        in_specs=[VMEM_SPEC] * 3,
        out_specs=[VMEM_SPEC] * 2,
        compiler_params=pltpu.CompilerParams(vmem_limit_bytes=4 * 2**20),
        cost_estimate=pl.CostEstimate(flops=2 * 10**11, bytes_accessed=10**9, transcendentals=0),
        name="forward",
    )(own, even, odd)


def lane_of(plane, b, c):
    if plane in (2, 3, 4) and -1 <= b <= 1:
        return PLANE_FIRST[plane] + THIN_FIRST[b + 3] + {-3: 0, -2: 1, -1: 2, 2: 2, 3: 3}[c]
    first = THIN_FIRST[b + 3] if plane in (2, 3, 4) else 7 * (b + 3)
    return PLANE_FIRST[plane] + first + c + 3


def window_of(window, one_window, own_ref, evenx_ref, oddx_ref, eveny_ref, oddy_ref):
    gx = lax.axis_index("gx")
    gy = lax.axis_index("gy")
    parity_x, parity_y = gx % 2, gy % 2
    even_x, odd_x = 6 * (1 - parity_x), 6 * parity_x
    even_y, odd_y = 6 * (1 - parity_y), 6 * parity_y
    one_even_x, one_odd_x = 1 + 4 * (1 - parity_x), 1 + 4 * parity_x
    one_even_y, one_odd_y = 1 + 4 * (1 - parity_y), 1 + 4 * parity_y

    end_x, end_y = lax.axis_size("gx") - 1, lax.axis_size("gy") - 1
    inner_x = jnp.where((gx == 0) | (gx == end_x), 0.0, 1.0)
    inner_y = jnp.where((gy == 0) | (gy == end_y), 0.0, 1.0)

    def put(x, y, block, factor=None):
        block = block.astype(F32)
        block = block if factor is None else block * factor
        window[x, y, 8:16, :] = block[0:8]
        window[x, y + 1, 8:16, :] = block[8:16]

    def put_one(x, y, block, factor=None):
        block = block.astype(F32)
        block = block if factor is None else block * factor
        for i in range(2):
            for j in range(2):
                first = (2 * i + j) * 4
                one_window[x + i, y + j, 8:12, :] = block[first:first + 4]

    for x in range(4):
        put(2 + x, 2, own_ref[x * 32:x * 32 + 16, :])
        put(2 + x, 4, own_ref[x * 32 + 16:x * 32 + 32, :])
    put_one(3, 3, own_ref[128:144, :])
    one = 1.0
    along_y = ((eveny_ref, even_y, one_even_y, one), (oddy_ref, odd_y, one_odd_y, inner_y))
    for got, y, one_y, factor in along_y:
        for x in range(4):
            put(2 + x, y, got[x * 16:x * 16 + 16, :], factor)
        put_one(3, one_y, got[64:80, :], factor)
    for got, place, one_x, factor_x in (
        (evenx_ref, even_x, one_even_x, one), (oddx_ref, odd_x, one_odd_x, inner_x)
    ):
        for x in range(2):
            put(place + x, 2, got[x * 32:x * 32 + 16, :], factor_x)
            put(place + x, 4, got[x * 32 + 16:x * 32 + 32, :], factor_x)
        put_one(one_x, 3, got[64:80, :], factor_x)
        for first, (_, y, one_y, factor_y) in zip((80, 128), along_y):
            for x in range(2):
                rows = slice(first + x * 16, first + x * 16 + 16)
                put(place + x, y, got[rows, :], factor_x * factor_y)
            put_one(one_x, one_y, got[first + 32:first + 48, :], factor_x * factor_y)


def translate_kernel(
    own_hbm, evenx_hbm, oddx_hbm, eveny_hbm, oddy_hbm,
    two_hbm, up_hbm, down_hbm, top_hbm, list_two_hbm, list_three_hbm, ops_hbm,
    out_ref, top_out,
    own_ref, evenx_ref, oddx_ref, eveny_ref, oddy_ref,
    two_ref, up_ref, down_ref, top_ref, list_two_ref, list_three_ref, fetch_sems,
    ops, window, one_window, chunks, one_chunks, high_chunks, two_rows, three_rows, acc,
    flags, one_local, sems,
):
    gx = lax.axis_index("gx")
    gy = lax.axis_index("gy")
    three_x, three_y = gx // 2, gy // 2
    copies = fetch(
        (own_hbm, evenx_hbm, oddx_hbm, eveny_hbm, oddy_hbm, two_hbm, up_hbm,
         list_two_hbm, list_three_hbm.at[three_x, three_y], down_hbm, top_hbm),
        (own_ref, evenx_ref, oddx_ref, eveny_ref, oddy_ref, two_ref, up_ref,
         list_two_ref, list_three_ref, down_ref, top_ref),
        fetch_sems,
    )
    def plane_copy(plane):
        span = pl.ds(PLANE_FIRST[plane], PLANE_COUNT[plane])
        return pltpu.make_async_copy(ops_hbm.at[span], ops.at[span], sems.at[plane])

    for plane in PLANE_ORDER[:2]:
        plane_copy(plane).start()

    window[:, :, 0:8, :] = jnp.zeros((8, 8, 8, PAIR), F32)
    window[:, :, 16:24, :] = jnp.zeros((8, 8, 8, PAIR), F32)
    one_window[...] = jnp.zeros_like(one_window)
    for copy in copies[:5]:
        copy.wait()
    window_of(window, one_window, own_ref, evenx_ref, oddx_ref, eveny_ref, oddy_ref)

    def fill(x, carry):
        for q in range(2):
            for d in range(3):
                for shift in range(3):
                    rows = pl.ds(7 + shift, 8)
                    both = [window[x, 2 * (y + d) + q, rows, :] for y in range(2)]
                    chunks[x, 3 * q + d, shift] = jnp.concatenate(both, axis=0).astype(BF16)
        return carry

    lax.fori_loop(0, 8, fill, 0)

    plane_copy(PLANE_ORDER[2]).start()
    for copy in copies[5:]:
        copy.wait()
    two_rows[...] = two_ref[...].astype(F32)
    cols = []
    for p in range(2):
        for q in range(2):
            for r in range(2):
                parts = []
                for x in range(4):
                    for z in range(2):
                        first = (2 * x + p) * 128 + q * 4 + 2 * z + r
                        parts.append(two_rows[pl.ds(first, 16, stride=8), :])
                cols.append(jnp.concatenate(parts, axis=0).astype(BF16))
    level_three = dot(jnp.concatenate(cols, axis=1), up_ref[...])
    three_rows[...] = level_three.astype(BF16).astype(F32)
    cols = []
    for p in range(2):
        for q in range(2):
            for r in range(2):
                parts = []
                for x in range(2):
                    first = ((2 * x + p) * 2 + r) * 16 + q
                    parts.append(three_rows[pl.ds(first, 8, stride=2), :])
                cols.append(jnp.concatenate(parts, axis=0).astype(BF16))
    top_out[...] = dot(jnp.concatenate(cols, axis=1), up_ref[...]).astype(BF16)

    flags[...] = jnp.zeros_like(flags)
    flags[0:4, :] = list_two_ref[...].astype(F32)
    flags[4:6, :] = list_three_ref[...].astype(F32)
    row = lax.broadcasted_iota(jnp.int32, (8, NOFF), 0)
    held = flags[...]
    moved = jnp.concatenate([jnp.zeros((8, 1), F32), held[:, :NOFF - 1]], axis=1)
    marked = jnp.where(row % 2 == 0, held, moved)
    row = lax.broadcasted_iota(jnp.int32, (8, COEF), 0)
    for plane in range(7):
        two_x = jnp.clip(gx + plane - 3, 0, 7)
        far_x = jnp.clip(three_x + plane - 3, 0, 3)
        for b in range(-3, 4):
            two_first = (two_x * 32 + jnp.clip(gy + b, 0, 31)) * 4
            far_first = far_x * 32 + jnp.clip(three_y + b, 0, 15)
            thin = plane in (2, 3, 4) and -1 <= b <= 1
            for r in range(2):
                low = two_rows[pl.ds(two_first + r, 1), :]
                high = two_rows[pl.ds(two_first + 2 + r, 1), :]
                far = three_rows[pl.ds(far_first + 16 * r, 1), :]
                low, high, far = (jnp.broadcast_to(v, (8, COEF)) for v in (low, high, far))
                near = jnp.where(row < 2, low, jnp.where(row < 4, high, far))
                for shift in range(3):
                    if thin and shift == 1:
                        continue
                    lane = lane_of(plane, b, 2 * (shift - 1) + r)
                    mark = jnp.broadcast_to(marked[:, lane:lane + 1], (8, COEF))
                    if shift == 0:
                        value = low
                    elif shift == 2:
                        value = high
                    else:
                        value = near
                    value = jnp.concatenate([value * mark, jnp.zeros((8, COEF), F32)], axis=0)
                    high_chunks[plane * 7 + b + 3, shift, :, r * COEF:r * COEF + COEF] = (
                        value.astype(BF16)
                    )

    acc[...] = jnp.zeros_like(acc)
    zero = jnp.zeros((COEF, COEF), BF16)

    def plane_step(plane, first, thin_plane, outer):
        a = plane - 3
        for b in range(-3, 4):
            for shift in range(3):
                for px in range(2):
                    for py in range(2):
                        rows = slice((2 * px + py) * 4, (2 * px + py) * 4 + 4)
                        one_chunks[b + 3, shift, rows, :] = one_window[
                            px + a + 3, py + b + 3, 7 + shift:11 + shift, :
                        ]
        parities = (jnp.where(a < 0, 1, 0),) if outer else (0, 1)
        places = [2 * x + px + a + 2 for px in parities for x in range(2)]
        size = 16 * len(places)
        totals = [None, None, None]
        for b in range(-3, 4):
            thin = thin_plane and -1 <= b <= 1
            start = first + (THIN_FIRST[b + 3] if thin_plane else 7 * (b + 3))
            sides = [py for py in range(2) if -2 <= b + py <= 3]
            left = []
            right = []
            for shift in (0, 2) if thin else (0, 1, 2):
                blocks = []
                for py in sides:
                    q, d = (py + b) % 2, (py + b) // 2 + 1
                    for place in places:
                        blocks.append(chunks[place, 3 * q + d, shift])
                blocks.append(one_chunks[b + 3, shift].astype(BF16))
                blocks.append(high_chunks[plane * 7 + b + 3, shift])
                left.append(jnp.concatenate(blocks, axis=0))
                if thin:
                    if shift == 0:
                        same, prev, after = ops[start + 1], ops[start], zero
                    else:
                        same, prev, after = ops[start + 2], zero, ops[start + 3]
                else:
                    c = 2 * (shift - 1) + 3
                    same, prev, after = ops[start + c], ops[start + c - 1], ops[start + c + 1]
                right.append(jnp.concatenate([same, prev], axis=1))
                right.append(jnp.concatenate([after, same], axis=1))
            product = dot(jnp.concatenate(left, axis=1), jnp.concatenate(right, axis=0))
            pieces = [product[i * size:(i + 1) * size] for i in range(len(sides))]
            pieces.append(product[len(sides) * size:])
            for side, piece in zip(sides + [2], pieces):
                totals[side] = piece if totals[side] is None else totals[side] + piece
        for side in range(2):
            if outer:
                rows = pl.ds(pl.multiple_of(side * 64 + parities[0] * 32, 32), 32)
            else:
                rows = slice(side * 64, side * 64 + 64)
            acc[rows, :] = acc[rows, :] + totals[side]
        acc[128:160, :] = acc[128:160, :] + totals[2]

    def thin_step(i, carry):
        first = 98 + 40 * i
        span = pl.ds(first, 40)
        pltpu.make_async_copy(ops_hbm.at[span], ops.at[span], sems.at[i + 2]).wait()
        ahead = pl.ds(jnp.where(i == 0, 49, jnp.where(i == 1, 218, 0)), 49)
        slot = jnp.where(i == 0, 1, jnp.where(i == 1, 5, 0))
        pltpu.make_async_copy(ops_hbm.at[ahead], ops.at[ahead], sems.at[slot]).start()
        plane_step(i + 2, first, True, False)
        return carry

    def wide_step(i, carry):
        plane = 1 + 4 * i
        first = 49 + 169 * i
        span = pl.ds(first, 49)
        pltpu.make_async_copy(ops_hbm.at[span], ops.at[span], sems.at[plane]).wait()
        plane_step(plane, first, False, False)
        return carry

    def outer_step(i, carry):
        plane = 6 * i
        first = 267 * i
        span = pl.ds(first, 49)
        pltpu.make_async_copy(ops_hbm.at[span], ops.at[span], sems.at[plane]).wait()
        plane_step(plane, first, False, True)
        return carry

    lax.fori_loop(0, 3, thin_step, 0)
    plane_copy(6).start()
    lax.fori_loop(0, 2, wide_step, 0)
    lax.fori_loop(0, 2, outer_step, 0)

    high = acc[144:152, :]
    top_x, top_y = three_x // 2, three_y // 2
    column = pl.multiple_of((three_x % 2 * 4 + three_y % 2 * 2) * COEF, PAIR)
    top_row = jnp.broadcast_to(top_ref[top_x, top_y], (8, COEF)).astype(BF16)
    three = dot(top_row, down_ref[:, pl.ds(column, PAIR)])
    row = lax.broadcasted_iota(jnp.int32, (8, COEF), 0)
    three_low = three[0:1, 0:COEF] + high[4:5, 0:COEF] * 0.125
    three_high = three[0:1, COEF:PAIR] + high[5:6, COEF:PAIR] * 0.125
    local_three = jnp.where(
        row == 0, jnp.broadcast_to(three_low, (8, COEF)), jnp.broadcast_to(three_high, (8, COEF))
    )
    column = pl.multiple_of((gx % 2 * 4 + gy % 2 * 2) * COEF, PAIR)
    two = dot(local_three.astype(BF16), down_ref[:, pl.ds(column, PAIR)])
    local_two = None
    for z in range(4):
        lanes = slice((z % 2) * COEF, (z % 2) * COEF + COEF)
        value = two[z // 2:z // 2 + 1, lanes] + high[z:z + 1, lanes] * 0.25
        value = jnp.broadcast_to(value, (8, COEF))
        local_two = value if local_two is None else jnp.where(row >= z, value, local_two)
    one = dot(local_two.astype(BF16), down_ref[...])
    one_mark = own_ref[272:288, :].astype(F32)
    for column in range(4):
        rows = slice(column * 4, column * 4 + 4)
        for r in range(2):
            lanes = slice(r * COEF, r * COEF + COEF)
            wide = slice((2 * column + r) * COEF, (2 * column + r) * COEF + COEF)
            far = acc[128 + column * 4:132 + column * 4, lanes] * one_mark[rows, lanes]
            one_local[pl.ds(column * 8 + r, 4, stride=2), :] = one[0:4, wide] + far * 0.5
    leaf = dot(one_local[...].astype(BF16), down_ref[...])
    leaf_mark = own_ref[144:272, :].astype(F32)
    for px in range(2):
        for py in range(2):
            for x in range(2):
                for y in range(2):
                    part = 8 * (2 * x + y)
                    held = ((2 * py + px) * 2 + x) * 16 + 8 * y
                    box_x, box_y = 2 * x + px, 2 * y + py
                    marked = box_x * 32 + box_y * 8
                    for r in range(2):
                        lanes = slice(r * COEF, r * COEF + COEF)
                        wide = slice((4 * px + 2 * py + r) * COEF, (4 * px + 2 * py + r + 1) * COEF)
                        mark = leaf_mark[marked:marked + 8, lanes]
                        out_ref[box_x, box_y, pl.ds(r, 8, stride=2), :] = (
                            leaf[part:part + 8, wide] + acc[held:held + 8, lanes] * mark
                        )


def translate(*operands):
    return pl.pallas_call(
        translate_kernel,
        out_shape=(
            jax.ShapeDtypeStruct((4, 4, 16, COEF), F32),
            jax.ShapeDtypeStruct((16, COEF), BF16),
        ),
        in_specs=[ANY_SPEC] * 12,
        out_specs=[VMEM_SPEC] * 2,
        scratch_shapes=[
            VM((288, PAIR), BF16),
            VM((176, PAIR), BF16),
            VM((176, PAIR), BF16),
            VM((80, PAIR), BF16),
            VM((80, PAIR), BF16),
            VM((1024, COEF), BF16),
            VM((1024, COEF), BF16),
            VM((COEF, 1024), BF16),
            VM((2, 8, 1, COEF), F32),
            VM((4, NOFF), jnp.int32),
            VM((2, NOFF), jnp.int32),
            pltpu.SemaphoreType.DMA((11,)),
            VM((NOFF, COEF, COEF), BF16),
            VM((8, 8, 24, PAIR), F32),
            VM((8, 8, 16, PAIR), F32),
            VM((8, 6, 3, 16, PAIR), BF16),
            VM((7, 3, 16, PAIR), F32),
            VM((49, 3, 16, PAIR), BF16),
            VM((1024, COEF), F32),
            VM((128, COEF), F32),
            VM((160, PAIR), F32),
            VM((8, NOFF), F32),
            VM((32, COEF), F32),
            pltpu.SemaphoreType.DMA((7,)),
        ],
        compiler_params=pltpu.CompilerParams(vmem_limit_bytes=int(LIM2 * 2**20)),
        name="translate",
    )(*operands)


def swaps(size_x, size_y):
    def odd(i):
        return ((i + 1) ^ 1) - 1

    every = [(x, y) for x in range(size_x) for y in range(size_y)]
    partners = (
        lambda x, y: (x ^ 1, y),
        lambda x, y: (odd(x) % size_x, y),
        lambda x, y: (x, y ^ 1),
        lambda x, y: (x, odd(y)) if 0 <= odd(y) < size_y else (x ^ 1, y),
    )
    place = lambda box: box[0] * size_y + box[1]
    return [[(place(box), place(partner(*box))) for box in every] for partner in partners]


def local(
    leaf_multipoles, top_local, upward_ops, downward_ops, translate_ops,
    interaction_leaf, interaction_one, interaction_two, interaction_three,
):
    count_x, count_y = lax.axis_size("gx"), lax.axis_size("gy")
    last = (1, 2, 3, 0)
    own, to_even, to_odd, two = prepare(
        count_x * count_y, leaf_multipoles, upward_ops, interaction_leaf.transpose(last), interaction_one.transpose(last)
    )
    axes = ("gx", "gy")
    pairs_even_x, pairs_odd_x, pairs_even_y, pairs_odd_y = swaps(count_x, count_y)
    even_y = lax.ppermute(to_even, axes, pairs_even_y)
    odd_y = lax.ppermute(to_odd, axes, pairs_odd_y)
    to_even, to_odd = forward(own, even_y, odd_y)
    even_x = lax.ppermute(to_even, axes, pairs_even_x)
    odd_x = lax.ppermute(to_odd, axes, pairs_odd_x)
    all_two = lax.all_to_all(two, axes, 0, 0, tiled=True).reshape(-1, COEF)
    leaf_local, top = translate(
        own, even_x, odd_x, even_y, odd_y,
        all_two, upward_ops, downward_ops, top_local,
        interaction_two.transpose(last).reshape(4, NOFF), interaction_three.transpose(last),
        translate_ops,
    )
    return leaf_local, top.reshape(2, 8, 1, COEF)


def solution(mesh):
    return jax.shard_map(
        local,
        mesh=mesh,
        in_specs=(
            P("gx", "gy", None, None),
            P(),
            P(),
            P(),
            P(),
            P(None, "gx", "gy", None),
            P(None, "gx", "gy", None),
            P(None, "gx", "gy", None),
            P(),
        ),
        out_specs=(P("gx", "gy", None, None), P()),
        check_vma=False,
    )
```

```python
import functools

import jax
import jax.numpy as jnp
from jax import lax
from jax.experimental import pallas as pl
from jax.experimental.pallas import tpu as pltpu
from jax.sharding import PartitionSpec as P

F32 = jnp.float32
BF16 = jnp.bfloat16
COEF = 128
PAIR = 256
NOFF = 316
VM = pltpu.VMEM
LIM1 = 60
LIM2 = 46
ANY_SPEC = pl.BlockSpec(memory_space=pl.ANY)
VMEM_SPEC = pl.BlockSpec(memory_space=pltpu.VMEM)

PLANE_FIRST = (0, 49, 98, 138, 178, 218, 267)
PLANE_COUNT = (49, 49, 40, 40, 40, 49, 49)
PLANE_ORDER = (2, 3, 4, 1, 5, 0, 6)
THIN_FIRST = (0, 7, 14, 18, 22, 26, 33)


def fetch(sources, targets, sems):
    copies = []
    for place, (source, target) in enumerate(zip(sources, targets)):
        copies.append(pltpu.make_async_copy(source, target, sems.at[place]))
        copies[-1].start()
    return copies


def dot(lhs, rhs):
    return jnp.dot(lhs, rhs, preferred_element_type=F32)


def prepare_kernel(
    leaf_hbm, up_hbm, list_leaf_hbm, list_one_hbm,
    own_out, even_out, odd_out, two_out,
    leaf_ref, up_ref, list_leaf_ref, list_one_ref,
    raw, masked, marks, one_raw, one_masked, one_marks, pairs, pair_marks, two_in, sems,
):
    copies = fetch(
        (leaf_hbm, list_leaf_hbm, up_hbm, list_one_hbm),
        (leaf_ref, list_leaf_ref, up_ref, list_one_ref),
        sems,
    )
    parity = lax.axis_index("gy") % 2
    copies[0].wait()
    copies[1].wait()
    for x in range(4):
        for y in range(4):
            rows = pl.ds((x * 4 + y) * 16, 16)
            flags = list_leaf_ref[x, y].astype(F32)
            mark = jnp.broadcast_to(jnp.max(flags, axis=1, keepdims=True), (16, COEF))
            value = leaf_ref[x, y].astype(F32)
            raw[rows, :] = value
            masked[rows, :] = value * mark
            marks[rows, :] = mark
    copies[2].wait()
    copies[3].wait()
    cols = []
    for p in range(2):
        for q in range(2):
            for r in range(2):
                parts = []
                for x in range(2):
                    for y in range(2):
                        first = ((2 * x + p) * 4 + 2 * y + q) * 16 + r
                        parts.append(raw[pl.ds(first, 8, stride=2), :])
                cols.append(jnp.concatenate(parts, axis=0).astype(BF16))
    level_one = dot(jnp.concatenate(cols, axis=1), up_ref[...]).astype(BF16).astype(F32)
    one_raw[...] = level_one
    for x in range(2):
        for y in range(2):
            rows = pl.ds((x * 2 + y) * 8, 8)
            flags = list_one_ref[x, y].astype(F32)
            mark = jnp.broadcast_to(jnp.max(flags, axis=1, keepdims=True), (8, COEF))
            one_masked[rows, :] = one_raw[rows, :] * mark
            one_marks[rows, :] = mark
    two_in[...] = jnp.zeros_like(two_in)
    for p in range(2):
        for q in range(2):
            for r in range(2):
                first = (p * 2 + q) * 8 + r
                lane = (4 * p + 2 * q + r) * COEF
                two_in[0:4, lane:lane + COEF] = one_raw[pl.ds(first, 4, stride=2), :]
    level_two = dot(two_in[...].astype(BF16), up_ref[...])
    two_out[...] = jnp.broadcast_to(level_two[0:4, :].astype(BF16)[None], two_out.shape)
    for x in range(4):
        for half in range(2):
            for r in range(2):
                lane = r * COEF
                parts = []
                part_marks = []
                for y in (2 * half, 2 * half + 1):
                    first = (x * 4 + y) * 16 + r
                    parts.append(masked[pl.ds(first, 8, stride=2), :])
                    part_marks.append(marks[pl.ds(first, 8, stride=2), :])
                first = x * 32 + half * 16
                rows = slice(first, first + 16)
                own_out[rows, lane:lane + COEF] = jnp.concatenate(parts, axis=0).astype(BF16)
                rows = slice(144 + first, 160 + first)
                own_out[rows, lane:lane + COEF] = jnp.concatenate(part_marks, axis=0).astype(BF16)
    for column in range(4):
        for r in range(2):
            lane = r * COEF
            rows = slice(column * 4, column * 4 + 4)
            pairs[rows, lane:lane + COEF] = one_masked[pl.ds(column * 8 + r, 4, stride=2), :]
            pair_marks[rows, lane:lane + COEF] = one_marks[pl.ds(column * 8 + r, 4, stride=2), :]
    one_pairs = pairs[...].astype(BF16)
    own_out[128:144, :] = one_pairs
    own_out[272:288, :] = pair_marks[...].astype(BF16)
    for out, side in ((even_out, 1 - parity), (odd_out, parity)):
        for x in range(4):
            rows = pl.ds(pl.multiple_of(x * 32 + side * 16, 16), 16)
            out[x * 16:x * 16 + 16, :] = own_out[rows, :]
    even_out[64:80, :] = one_pairs
    odd_out[64:80, :] = one_pairs


def prepare(receivers, leaf, upward_ops, list_leaf, list_one):
    return pl.pallas_call(
        prepare_kernel,
        out_shape=(
            jax.ShapeDtypeStruct((288, PAIR), BF16),
            jax.ShapeDtypeStruct((80, PAIR), BF16),
            jax.ShapeDtypeStruct((80, PAIR), BF16),
            jax.ShapeDtypeStruct((receivers, 4, COEF), BF16),
        ),
        in_specs=[ANY_SPEC] * 4,
        out_specs=[VMEM_SPEC] * 4,
        scratch_shapes=[
            VM((4, 4, 16, COEF), BF16),
            VM((1024, COEF), BF16),
            VM((4, 4, 16, NOFF), jnp.int32),
            VM((2, 2, 8, NOFF), jnp.int32),
            VM((256, COEF), F32),
            VM((256, COEF), F32),
            VM((256, COEF), F32),
            VM((32, COEF), F32),
            VM((32, COEF), F32),
            VM((32, COEF), F32),
            VM((16, PAIR), F32),
            VM((16, PAIR), F32),
            VM((8, 1024), F32),
            pltpu.SemaphoreType.DMA((4,)),
        ],
        compiler_params=pltpu.CompilerParams(vmem_limit_bytes=int(LIM1 * 2**20)),
        name="prepare",
    )(leaf, upward_ops, list_leaf, list_one)


def forward_kernel(own_ref, even_ref, odd_ref, even_out, odd_out):
    parity = lax.axis_index("gx") % 2
    for out, side in ((even_out, 1 - parity), (odd_out, parity)):
        out[0:64, :] = own_ref[pl.ds(pl.multiple_of(side * 64, 64), 64), :]
        out[64:80, :] = own_ref[128:144, :]
        for first, got in ((80, even_ref), (128, odd_ref)):
            out[first:first + 32, :] = got[pl.ds(pl.multiple_of(side * 32, 32), 32), :]
            out[first + 32:first + 48, :] = got[64:80, :]


def forward(own, even, odd):
    return pl.pallas_call(
        forward_kernel,
        out_shape=(jax.ShapeDtypeStruct((176, PAIR), BF16),) * 2,
        in_specs=[VMEM_SPEC] * 3,
        out_specs=[VMEM_SPEC] * 2,
        compiler_params=pltpu.CompilerParams(vmem_limit_bytes=4 * 2**20),
        cost_estimate=pl.CostEstimate(flops=10**11, bytes_accessed=0, transcendentals=0),
        name="forward",
    )(own, even, odd)


def lane_of(plane, b, c):
    if plane in (2, 3, 4) and -1 <= b <= 1:
        return PLANE_FIRST[plane] + THIN_FIRST[b + 3] + {-3: 0, -2: 1, -1: 2, 2: 2, 3: 3}[c]
    first = THIN_FIRST[b + 3] if plane in (2, 3, 4) else 7 * (b + 3)
    return PLANE_FIRST[plane] + first + c + 3


def window_of(window, one_window, own_ref, evenx_ref, oddx_ref, eveny_ref, oddy_ref):
    gx = lax.axis_index("gx")
    gy = lax.axis_index("gy")
    parity_x, parity_y = gx % 2, gy % 2
    even_x, odd_x = 6 * (1 - parity_x), 6 * parity_x
    even_y, odd_y = 6 * (1 - parity_y), 6 * parity_y
    one_even_x, one_odd_x = 1 + 4 * (1 - parity_x), 1 + 4 * parity_x
    one_even_y, one_odd_y = 1 + 4 * (1 - parity_y), 1 + 4 * parity_y

    end_x, end_y = lax.axis_size("gx") - 1, lax.axis_size("gy") - 1
    inner_x = jnp.where((gx == 0) | (gx == end_x), 0.0, 1.0)
    inner_y = jnp.where((gy == 0) | (gy == end_y), 0.0, 1.0)

    def put(x, y, block, factor=None):
        block = block.astype(F32)
        block = block if factor is None else block * factor
        window[x, y, 8:16, :] = block[0:8]
        window[x, y + 1, 8:16, :] = block[8:16]

    def put_one(x, y, block, factor=None):
        block = block.astype(F32)
        block = block if factor is None else block * factor
        for i in range(2):
            for j in range(2):
                first = (2 * i + j) * 4
                one_window[x + i, y + j, 8:12, :] = block[first:first + 4]

    for x in range(4):
        put(2 + x, 2, own_ref[x * 32:x * 32 + 16, :])
        put(2 + x, 4, own_ref[x * 32 + 16:x * 32 + 32, :])
    put_one(3, 3, own_ref[128:144, :])
    one = 1.0
    along_y = ((eveny_ref, even_y, one_even_y, one), (oddy_ref, odd_y, one_odd_y, inner_y))
    for got, y, one_y, factor in along_y:
        for x in range(4):
            put(2 + x, y, got[x * 16:x * 16 + 16, :], factor)
        put_one(3, one_y, got[64:80, :], factor)
    for got, place, one_x, factor_x in (
        (evenx_ref, even_x, one_even_x, one), (oddx_ref, odd_x, one_odd_x, inner_x)
    ):
        for x in range(2):
            put(place + x, 2, got[x * 32:x * 32 + 16, :], factor_x)
            put(place + x, 4, got[x * 32 + 16:x * 32 + 32, :], factor_x)
        put_one(one_x, 3, got[64:80, :], factor_x)
        for first, (_, y, one_y, factor_y) in zip((80, 128), along_y):
            for x in range(2):
                rows = slice(first + x * 16, first + x * 16 + 16)
                put(place + x, y, got[rows, :], factor_x * factor_y)
            put_one(one_x, one_y, got[first + 32:first + 48, :], factor_x * factor_y)


def translate_kernel(
    own_ref, evenx_ref, oddx_ref, eveny_ref, oddy_ref,
    two_ref, up_ref, down_ref, top_ref, list_two_ref, list_three_ref, ops_hbm,
    out_ref, top_out,
    ops, window, one_window, chunks, one_chunks, high_chunks, two_rows, three_rows, acc,
    flags, one_local, sems,
):
    gx = lax.axis_index("gx")
    gy = lax.axis_index("gy")
    three_x, three_y = gx // 2, gy // 2
    def plane_copy(plane):
        span = pl.ds(PLANE_FIRST[plane], PLANE_COUNT[plane])
        return pltpu.make_async_copy(ops_hbm.at[span], ops.at[span], sems.at[plane])

    for plane in PLANE_ORDER[:2]:
        plane_copy(plane).start()

    window[:, :, 0:8, :] = jnp.zeros((8, 8, 8, PAIR), F32)
    window[:, :, 16:24, :] = jnp.zeros((8, 8, 8, PAIR), F32)
    one_window[...] = jnp.zeros_like(one_window)
    window_of(window, one_window, own_ref, evenx_ref, oddx_ref, eveny_ref, oddy_ref)

    def fill(x, carry):
        for q in range(2):
            for d in range(3):
                for shift in range(3):
                    rows = pl.ds(7 + shift, 8)
                    both = [window[x, 2 * (y + d) + q, rows, :] for y in range(2)]
                    chunks[x, 3 * q + d, shift] = jnp.concatenate(both, axis=0).astype(BF16)
        return carry

    lax.fori_loop(0, 8, fill, 0)

    plane_copy(PLANE_ORDER[2]).start()
    two_rows[...] = two_ref[...].astype(F32)
    cols = []
    for p in range(2):
        for q in range(2):
            for r in range(2):
                parts = []
                for x in range(4):
                    for z in range(2):
                        first = (2 * x + p) * 128 + q * 4 + 2 * z + r
                        parts.append(two_rows[pl.ds(first, 16, stride=8), :])
                cols.append(jnp.concatenate(parts, axis=0).astype(BF16))
    level_three = dot(jnp.concatenate(cols, axis=1), up_ref[...])
    three_rows[...] = level_three.astype(BF16).astype(F32)
    cols = []
    for p in range(2):
        for q in range(2):
            for r in range(2):
                parts = []
                for x in range(2):
                    first = ((2 * x + p) * 2 + r) * 16 + q
                    parts.append(three_rows[pl.ds(first, 8, stride=2), :])
                cols.append(jnp.concatenate(parts, axis=0).astype(BF16))
    top_out[...] = dot(jnp.concatenate(cols, axis=1), up_ref[...]).astype(BF16)

    flags[...] = jnp.zeros_like(flags)
    flags[0:4, :] = list_two_ref[...].astype(F32)
    flags[4:6, :] = list_three_ref[three_x, three_y].astype(F32)
    row = lax.broadcasted_iota(jnp.int32, (8, NOFF), 0)
    held = flags[...]
    moved = jnp.concatenate([jnp.zeros((8, 1), F32), held[:, :NOFF - 1]], axis=1)
    marked = jnp.where(row % 2 == 0, held, moved)
    row = lax.broadcasted_iota(jnp.int32, (8, COEF), 0)
    for plane in range(7):
        two_x = jnp.clip(gx + plane - 3, 0, 7)
        far_x = jnp.clip(three_x + plane - 3, 0, 3)
        for b in range(-3, 4):
            two_first = (two_x * 32 + jnp.clip(gy + b, 0, 31)) * 4
            far_first = far_x * 32 + jnp.clip(three_y + b, 0, 15)
            thin = plane in (2, 3, 4) and -1 <= b <= 1
            for r in range(2):
                low = two_rows[pl.ds(two_first + r, 1), :]
                high = two_rows[pl.ds(two_first + 2 + r, 1), :]
                far = three_rows[pl.ds(far_first + 16 * r, 1), :]
                low, high, far = (jnp.broadcast_to(v, (8, COEF)) for v in (low, high, far))
                near = jnp.where(row < 2, low, jnp.where(row < 4, high, far))
                for shift in range(3):
                    if thin and shift == 1:
                        continue
                    lane = lane_of(plane, b, 2 * (shift - 1) + r)
                    mark = jnp.broadcast_to(marked[:, lane:lane + 1], (8, COEF))
                    if shift == 0:
                        value = low
                    elif shift == 2:
                        value = high
                    else:
                        value = near
                    value = jnp.concatenate([value * mark, jnp.zeros((8, COEF), F32)], axis=0)
                    high_chunks[plane * 7 + b + 3, shift, :, r * COEF:r * COEF + COEF] = (
                        value.astype(BF16)
                    )

    acc[...] = jnp.zeros_like(acc)
    zero = jnp.zeros((COEF, COEF), BF16)

    def plane_step(plane, first, thin_plane, outer):
        a = plane - 3
        for b in range(-3, 4):
            for shift in range(3):
                for px in range(2):
                    for py in range(2):
                        rows = slice((2 * px + py) * 4, (2 * px + py) * 4 + 4)
                        one_chunks[b + 3, shift, rows, :] = one_window[
                            px + a + 3, py + b + 3, 7 + shift:11 + shift, :
                        ]
        parities = (jnp.where(a < 0, 1, 0),) if outer else (0, 1)
        places = [2 * x + px + a + 2 for px in parities for x in range(2)]
        size = 16 * len(places)
        totals = [None, None, None]
        for b in range(-3, 4):
            thin = thin_plane and -1 <= b <= 1
            start = first + (THIN_FIRST[b + 3] if thin_plane else 7 * (b + 3))
            sides = [py for py in range(2) if -2 <= b + py <= 3]
            left = []
            right = []
            for shift in (0, 2) if thin else (0, 1, 2):
                blocks = []
                for py in sides:
                    q, d = (py + b) % 2, (py + b) // 2 + 1
                    for place in places:
                        blocks.append(chunks[place, 3 * q + d, shift])
                blocks.append(one_chunks[b + 3, shift].astype(BF16))
                blocks.append(high_chunks[plane * 7 + b + 3, shift])
                left.append(jnp.concatenate(blocks, axis=0))
                if thin:
                    if shift == 0:
                        same, prev, after = ops[start + 1], ops[start], zero
                    else:
                        same, prev, after = ops[start + 2], zero, ops[start + 3]
                else:
                    c = 2 * (shift - 1) + 3
                    same, prev, after = ops[start + c], ops[start + c - 1], ops[start + c + 1]
                right.append(jnp.concatenate([same, prev], axis=1))
                right.append(jnp.concatenate([after, same], axis=1))
            product = dot(jnp.concatenate(left, axis=1), jnp.concatenate(right, axis=0))
            pieces = [product[i * size:(i + 1) * size] for i in range(len(sides))]
            pieces.append(product[len(sides) * size:])
            for side, piece in zip(sides + [2], pieces):
                totals[side] = piece if totals[side] is None else totals[side] + piece
        for side in range(2):
            if outer:
                rows = pl.ds(pl.multiple_of(side * 64 + parities[0] * 32, 32), 32)
            else:
                rows = slice(side * 64, side * 64 + 64)
            acc[rows, :] = acc[rows, :] + totals[side]
        acc[128:160, :] = acc[128:160, :] + totals[2]

    def thin_step(i, carry):
        first = 98 + 40 * i
        span = pl.ds(first, 40)
        pltpu.make_async_copy(ops_hbm.at[span], ops.at[span], sems.at[i + 2]).wait()
        ahead = pl.ds(jnp.where(i == 0, 49, jnp.where(i == 1, 218, 0)), 49)
        slot = jnp.where(i == 0, 1, jnp.where(i == 1, 5, 0))
        pltpu.make_async_copy(ops_hbm.at[ahead], ops.at[ahead], sems.at[slot]).start()
        plane_step(i + 2, first, True, False)
        return carry

    def wide_step(i, carry):
        plane = 1 + 4 * i
        first = 49 + 169 * i
        span = pl.ds(first, 49)
        pltpu.make_async_copy(ops_hbm.at[span], ops.at[span], sems.at[plane]).wait()
        plane_step(plane, first, False, False)
        return carry

    def outer_step(i, carry):
        plane = 6 * i
        first = 267 * i
        span = pl.ds(first, 49)
        pltpu.make_async_copy(ops_hbm.at[span], ops.at[span], sems.at[plane]).wait()
        plane_step(plane, first, False, True)
        return carry

    lax.fori_loop(0, 3, thin_step, 0)
    plane_copy(6).start()
    lax.fori_loop(0, 2, wide_step, 0)
    lax.fori_loop(0, 2, outer_step, 0)

    high = acc[144:152, :]
    top_x, top_y = three_x // 2, three_y // 2
    column = pl.multiple_of((three_x % 2 * 4 + three_y % 2 * 2) * COEF, PAIR)
    top_row = jnp.broadcast_to(top_ref[top_x, top_y], (8, COEF)).astype(BF16)
    three = dot(top_row, down_ref[:, pl.ds(column, PAIR)])
    row = lax.broadcasted_iota(jnp.int32, (8, COEF), 0)
    three_low = three[0:1, 0:COEF] + high[4:5, 0:COEF] * 0.125
    three_high = three[0:1, COEF:PAIR] + high[5:6, COEF:PAIR] * 0.125
    local_three = jnp.where(
        row == 0, jnp.broadcast_to(three_low, (8, COEF)), jnp.broadcast_to(three_high, (8, COEF))
    )
    column = pl.multiple_of((gx % 2 * 4 + gy % 2 * 2) * COEF, PAIR)
    two = dot(local_three.astype(BF16), down_ref[:, pl.ds(column, PAIR)])
    local_two = None
    for z in range(4):
        lanes = slice((z % 2) * COEF, (z % 2) * COEF + COEF)
        value = two[z // 2:z // 2 + 1, lanes] + high[z:z + 1, lanes] * 0.25
        value = jnp.broadcast_to(value, (8, COEF))
        local_two = value if local_two is None else jnp.where(row >= z, value, local_two)
    one = dot(local_two.astype(BF16), down_ref[...])
    one_mark = own_ref[272:288, :].astype(F32)
    for column in range(4):
        rows = slice(column * 4, column * 4 + 4)
        for r in range(2):
            lanes = slice(r * COEF, r * COEF + COEF)
            wide = slice((2 * column + r) * COEF, (2 * column + r) * COEF + COEF)
            far = acc[128 + column * 4:132 + column * 4, lanes] * one_mark[rows, lanes]
            one_local[pl.ds(column * 8 + r, 4, stride=2), :] = one[0:4, wide] + far * 0.5
    leaf = dot(one_local[...].astype(BF16), down_ref[...])
    leaf_mark = own_ref[144:272, :].astype(F32)
    for px in range(2):
        for py in range(2):
            for x in range(2):
                for y in range(2):
                    part = 8 * (2 * x + y)
                    held = ((2 * py + px) * 2 + x) * 16 + 8 * y
                    box_x, box_y = 2 * x + px, 2 * y + py
                    marked = box_x * 32 + box_y * 8
                    for r in range(2):
                        lanes = slice(r * COEF, r * COEF + COEF)
                        wide = slice((4 * px + 2 * py + r) * COEF, (4 * px + 2 * py + r + 1) * COEF)
                        mark = leaf_mark[marked:marked + 8, lanes]
                        out_ref[box_x, box_y, pl.ds(r, 8, stride=2), :] = (
                            leaf[part:part + 8, wide] + acc[held:held + 8, lanes] * mark
                        )


def translate(*operands):
    return pl.pallas_call(
        translate_kernel,
        out_shape=(
            jax.ShapeDtypeStruct((4, 4, 16, COEF), F32),
            jax.ShapeDtypeStruct((16, COEF), BF16),
        ),
        in_specs=[VMEM_SPEC] * 11 + [ANY_SPEC],
        out_specs=[VMEM_SPEC] * 2,
        scratch_shapes=[
            VM((NOFF, COEF, COEF), BF16),
            VM((8, 8, 24, PAIR), F32),
            VM((8, 8, 16, PAIR), F32),
            VM((8, 6, 3, 16, PAIR), BF16),
            VM((7, 3, 16, PAIR), F32),
            VM((49, 3, 16, PAIR), BF16),
            VM((1024, COEF), F32),
            VM((128, COEF), F32),
            VM((160, PAIR), F32),
            VM((8, NOFF), F32),
            VM((32, COEF), F32),
            pltpu.SemaphoreType.DMA((7,)),
        ],
        compiler_params=pltpu.CompilerParams(vmem_limit_bytes=int(LIM2 * 2**20)),
        name="translate",
    )(*operands)


def swaps(size_x, size_y):
    def odd(i):
        return ((i + 1) ^ 1) - 1

    every = [(x, y) for x in range(size_x) for y in range(size_y)]
    partners = (
        lambda x, y: (x ^ 1, y),
        lambda x, y: (odd(x) % size_x, y),
        lambda x, y: (x, y ^ 1),
        lambda x, y: (x, odd(y)) if 0 <= odd(y) < size_y else (x ^ 1, y),
    )
    place = lambda box: box[0] * size_y + box[1]
    return [[(place(box), place(partner(*box))) for box in every] for partner in partners]


def local(
    leaf_multipoles, top_local, upward_ops, downward_ops, translate_ops,
    interaction_leaf, interaction_one, interaction_two, interaction_three,
):
    count_x, count_y = lax.axis_size("gx"), lax.axis_size("gy")
    last = (1, 2, 3, 0)
    own, to_even, to_odd, two = prepare(
        count_x * count_y, leaf_multipoles, upward_ops, interaction_leaf.transpose(last), interaction_one.transpose(last)
    )
    axes = ("gx", "gy")
    pairs_even_x, pairs_odd_x, pairs_even_y, pairs_odd_y = swaps(count_x, count_y)
    even_y = lax.ppermute(to_even, axes, pairs_even_y)
    odd_y = lax.ppermute(to_odd, axes, pairs_odd_y)
    to_even, to_odd = forward(own, even_y, odd_y)
    even_x = lax.ppermute(to_even, axes, pairs_even_x)
    odd_x = lax.ppermute(to_odd, axes, pairs_odd_x)
    all_two = lax.all_to_all(two, axes, 0, 0, tiled=True).reshape(-1, COEF)
    leaf_local, top = translate(
        own, even_x, odd_x, even_y, odd_y,
        all_two, upward_ops, downward_ops, top_local,
        interaction_two.transpose(last).reshape(4, NOFF), interaction_three.transpose(last),
        translate_ops,
    )
    return leaf_local, top.reshape(2, 8, 1, COEF)


def solution(mesh):
    return jax.shard_map(
        local,
        mesh=mesh,
        in_specs=(
            P("gx", "gy", None, None),
            P(),
            P(),
            P(),
            P(),
            P(None, "gx", "gy", None),
            P(None, "gx", "gy", None),
            P(None, "gx", "gy", None),
            P(),
        ),
        out_specs=(P("gx", "gy", None, None), P()),
        check_vma=False,
    )
```
